32 devices in a mesh: outer: 8 (over z, y), inner: 4 (over x, core).
Axes of the slice: x: 2, y: 2, z: 4, core: 2. Of those that a mesh axis runs over, the one named last changes fastest.
Arguments:
- image_embeds: bfloat16 [16384, 512], P(('outer', 'inner')), may hold values from -0.17766058 to 0.17766058
- text_embeds: bfloat16 [16384, 512], P(('outer', 'inner')), may hold values from -0.17766058 to 0.17766058
- image_lse: float32 [16384], P(('outer', 'inner')), as said below
- text_lse: float32 [16384], P(('outer', 'inner')), as said below
- logit_scale: float32 [], replicated, may hold values from 90 to 100, as said below
Outputs:
- image_grad: float32 [16384, 512], P(('outer', 'inner'))
- text_grad: float32 [16384, 512], P(('outer', 'inner'))
The draws below stay inside these ranges and needn't reach their ends.
Inputs may be any that keep to these rules, and one draw needn't show every extreme that they name: logit_scale is one positive number. `image_lse`: saved by the forward pass: for image row i, the log of the sum of exp(score_ij) over the text rows j that the window pairs with it. `text_lse`: saved by the forward pass: for text row j, the log of the sum of exp(score_ij) over the image rows i that the window pairs with it.
All inputs are finite; a program needn't handle non-finite values.
Results may differ from the reference program's by a relative error of at most 0.0013.
Values may be sent and summed in bfloat16 or wider, within the bound.
A program may use at most 64 MiB of HBM per device.

```python
import math
import jax
import jax.numpy as jnp
from jax import lax

E = 512
ROWS = 512
PAIRS = 16384
N_OUTER = 8
N_INNER = 4


def shared_scale(key):
    return 90.0 + 10.0 * jax.random.uniform(jax.random.fold_in(key, 97), (), jnp.float32)


def modality(key, label_id, exponent):
    key = jax.random.fold_in(key, label_id)
    normal_draw = jax.random.normal(key, (PAIRS, E), jnp.float32)
    shaped = jnp.sign(normal_draw) * jnp.abs(normal_draw) ** exponent
    blended = shaped
    return (jnp.clip(blended, -4.0, 4.0) * (1.0 / math.sqrt(E))).astype(jnp.bfloat16)


def window_lse(key, exponent):
    factor = shared_scale(key)
    images = lax.optimization_barrier(modality(key, 101, exponent)).astype(jnp.float32)
    text_rows = lax.optimization_barrier(modality(key, 202, exponent)).astype(jnp.float32)
    images = images.reshape(N_OUTER, N_INNER, ROWS, E)
    text_rows = text_rows.reshape(N_OUTER, N_INNER, ROWS, E)
    left_text = jnp.roll(text_rows, 1, axis=1)
    upper_text = jnp.roll(text_rows, 1, axis=0)
    corner_text = jnp.roll(upper_text, 1, axis=1)

    def one_group(inputs):
        image_block = inputs[0]
        score_tiles = jnp.stack([factor * jnp.einsum('nre,nse->nrs', image_block, text_block, precision=lax.Precision.HIGHEST) for text_block in inputs[1:]], axis=1)
        return (jax.nn.logsumexp(score_tiles, axis=(1, 3)), jax.nn.logsumexp(score_tiles, axis=2))
    row_lse, column_lse = lax.map(one_group, (images, text_rows, left_text, upper_text, corner_text))
    column_parts = jnp.stack([column_lse[:, :, 0], jnp.roll(column_lse[:, :, 1], -1, axis=1), jnp.roll(column_lse[:, :, 2], -1, axis=0), jnp.roll(jnp.roll(column_lse[:, :, 3], -1, axis=0), -1, axis=1)], axis=0)
    text_stat = jax.nn.logsumexp(column_parts, axis=0)
    return (row_lse.reshape(PAIRS), text_stat.reshape(PAIRS))


def draw_logit_scale(key, part):
    return shared_scale(key).astype(jnp.float32)


def draw_image_embeds(key, part):
    return modality(key, 101, 1.0)


def draw_text_embeds(key, part):
    return modality(key, 202, 1.0)


def draw_image_lse(key, part):
    row_lse, text_stat = window_lse(key, 1.0)
    return row_lse.astype(jnp.float32)


def draw_text_lse(key, part):
    row_lse, text_stat = window_lse(key, 1.0)
    return text_stat.astype(jnp.float32)


def setup_inputs(seed: int = 0) -> dict:
    arg_keys = jax.random.split(jax.random.key(seed), 6)
    image_embeds = draw_image_embeds(jax.random.fold_in(arg_keys[5], 71), 0)
    text_embeds = draw_text_embeds(jax.random.fold_in(arg_keys[5], 71), 0)
    image_lse = draw_image_lse(jax.random.fold_in(arg_keys[5], 71), 0)
    text_lse = draw_text_lse(jax.random.fold_in(arg_keys[5], 71), 0)
    logit_scale = draw_logit_scale(jax.random.fold_in(arg_keys[5], 71), 0)
    return dict(image_embeds=image_embeds, text_embeds=text_embeds, image_lse=image_lse, text_lse=text_lse, logit_scale=logit_scale)


def tile_terms(images, image_stat, text_rows, text_stat, factor):
    scores = factor * jnp.einsum("nre,nse->nrs", images.astype(jnp.float32), text_rows.astype(jnp.float32))
    weights = (jnp.exp(scores - image_stat[:, :, None]) + jnp.exp(scores - text_stat[:, None, :])).astype(jnp.bfloat16)
    widened = lax.optimization_barrier(weights).astype(jnp.float32)
    image_term = jnp.einsum("nrs,nse->nre", widened, text_rows.astype(jnp.float32))
    text_term = jnp.einsum("nrs,nre->nse", widened, images.astype(jnp.float32))
    return image_term, text_term


def reference(image_embeds, text_embeds, image_lse, text_lse, logit_scale):
    factor = logit_scale.astype(jnp.float32)
    images = image_embeds.reshape(N_OUTER, N_INNER, ROWS, E)
    text_rows = text_embeds.reshape(N_OUTER, N_INNER, ROWS, E)
    image_stat = image_lse.astype(jnp.float32).reshape(N_OUTER, N_INNER, ROWS)
    text_stat = text_lse.astype(jnp.float32).reshape(N_OUTER, N_INNER, ROWS)
    left_text = jnp.roll(text_rows, 1, axis=1)
    upper_text = jnp.roll(text_rows, 1, axis=0)
    corner_text = jnp.roll(upper_text, 1, axis=1)
    left_stat = jnp.roll(text_stat, 1, axis=1)
    upper_stat = jnp.roll(text_stat, 1, axis=0)
    corner_stat = jnp.roll(upper_stat, 1, axis=1)

    def one_group(inputs):
        image_block, image_here, own_text, own_stat, left_block, left_here, upper_block, upper_here, corner_block, corner_here = inputs
        own_image, own_part = tile_terms(image_block, image_here, own_text, own_stat, factor)
        left_image, left_part = tile_terms(image_block, image_here, left_block, left_here, factor)
        upper_image, upper_part = tile_terms(image_block, image_here, upper_block, upper_here, factor)
        corner_image, corner_part = tile_terms(image_block, image_here, corner_block, corner_here, factor)
        image_total = own_image + left_image + upper_image + corner_image
        same_group = own_part + jnp.roll(left_part, -1, axis=0)
        prior_group = upper_part + jnp.roll(corner_part, -1, axis=0)
        return image_total, same_group, prior_group

    image_total, same_group, prior_group = lax.map(one_group, (images, image_stat, text_rows, text_stat, left_text, left_stat, upper_text, upper_stat, corner_text, corner_stat))
    text_total = same_group + jnp.roll(prior_group, -1, axis=0)
    image_grad = factor * (image_total - 2.0 * text_rows.astype(jnp.float32))
    text_grad = factor * (text_total - 2.0 * images.astype(jnp.float32))
    return image_grad.reshape(PAIRS, E), text_grad.reshape(PAIRS, E)
```

```python
import functools
import math

import jax
import jax.numpy as jnp
from jax import lax
from jax.experimental import pallas as pl
from jax.experimental.pallas import tpu as pltpu
from jax.sharding import PartitionSpec as P

MESH = pl.DeviceIdType.MESH
LOG2E = math.log2(math.e)
LANES = 128
NEAR, FAR, BOTH = 0, 1, 2
NT = (((1,), (1,)), ((), ()))


def kernel(
    piece,
    scale_ref,
    images_ref,
    texts_ref,
    image_lse_ref,
    text_lse_ref,
    image_grad_ref,
    text_grad_ref,
    held,
    stat,
    column,
    got,
    got_stat,
    total,
    load_sem,
    send_sem,
    recv_sem,
    stat_send_sem,
    stat_recv_sem,
    out_sem,
):
    rows, width = images_ref.shape
    pieces = rows // piece
    outer, inner = lax.axis_index("outer"), lax.axis_index("inner")
    n_outer, n_inner = lax.axis_size("outer"), lax.axis_size("inner")
    scale = scale_ref[0, 0]
    factor = scale * LOG2E

    loads = [
        pltpu.make_async_copy(source, target, load_sem.at[index])
        for index, (source, target) in enumerate(
            [
                (texts_ref, held.at[0]),
                (images_ref, held.at[1]),
                (text_lse_ref, stat.at[0]),
                (image_lse_ref, stat.at[1]),
            ]
        )
    ]
    for load in loads:
        load.start()

    barrier = pltpu.get_barrier_semaphore()
    for step in (1, -1):
        pl.semaphore_signal(
            barrier, inc=1, device_id={"outer": (outer + step + n_outer) % n_outer},
            device_id_type=MESH,
        )
        pl.semaphore_signal(
            barrier, inc=1, device_id={"inner": (inner + step + n_inner) % n_inner},
            device_id_type=MESH,
        )
    pl.semaphore_wait(barrier, 4)
    for load in loads:
        load.wait()

    side_a = 1 - inner % 2
    side_b = inner % 2

    def target(kind, side):
        step = 1 - 2 * side
        if kind == FAR:
            return {"outer": (outer + step + n_outer) % n_outer}
        return {"inner": (inner + step + n_inner) % n_inner}

    def span(c):
        return pl.ds(pl.multiple_of(c * piece, piece), piece)

    def block_copy(kind, side, c):
        source = got.at[FAR, side, span(c)] if kind == BOTH else held.at[side, span(c)]
        return pltpu.make_async_remote_copy(
            src_ref=source,
            dst_ref=got.at[kind, side, span(c)],
            send_sem=send_sem.at[kind, side, c],
            recv_sem=recv_sem.at[kind, side, c],
            device_id=target(kind, side),
            device_id_type=MESH,
        )

    def stat_copy(kind, side):
        source = got_stat.at[FAR, side] if kind == BOTH else stat.at[side]
        return pltpu.make_async_remote_copy(
            src_ref=source,
            dst_ref=got_stat.at[kind, side],
            send_sem=stat_send_sem.at[kind, side],
            recv_sem=stat_recv_sem.at[kind, side],
            device_id=target(kind, side),
            device_id_type=MESH,
        )

    def for_pieces(body):
        def step(c, carry):
            body(c)
            return carry

        lax.fori_loop(0, pieces, step, 0)

    for side in (side_a, side_b):
        for kind in (FAR, NEAR):
            stat_copy(kind, side).start()

    def send_first(c):
        block_copy(FAR, side_a, c).start()
        block_copy(NEAR, side_a, c).start()

    def send_near(c):
        block_copy(NEAR, side_b, c).start()

    def send_far(c):
        block_copy(FAR, side_b, c).start()

    for_pieces(send_first)
    for_pieces(send_near)
    for_pieces(send_far)

    for side in (0, 1):
        column[side] = jnp.broadcast_to(stat[side] * LOG2E, (LANES, rows)).T

    def contribution(side, start, size, block, row):
        scores = factor * lax.dot_general(
            held[1 - side, pl.ds(start, size), :], block, NT,
            preferred_element_type=jnp.float32,
        )
        wide = jnp.concatenate(
            [column[1 - side, pl.ds(start, size), :]] * (block.shape[0] // LANES), axis=1
        )
        weights = (jnp.exp2(scores - wide) + jnp.exp2(scores - row)).astype(jnp.bfloat16)
        return jnp.dot(weights, block, preferred_element_type=jnp.float32)

    band = 256

    def add_piece(kind, side, c):
        block = got[kind, side, span(c), :]
        row = got_stat[kind, side, :, span(c)] * LOG2E
        for start in range(0, rows, band):
            total[side, pl.ds(start, band), :] += contribution(side, start, band, block, row)

    for side in (0, 1):
        block = held[side]
        row = stat[side] * LOG2E
        for start in range(0, rows, band):
            total[side, pl.ds(start, band), :] = contribution(side, start, band, block, row)

    def receive(kind, side, c):
        block_copy(kind, side, c).wait_recv()

    stat_copy(NEAR, side_a).wait_recv()

    def near_a(c):
        receive(NEAR, side_a, c)
        add_piece(NEAR, side_a, c)

    for_pieces(near_a)

    for side in (side_a, side_b):
        stat_copy(FAR, side).wait_recv()
        stat_copy(BOTH, side).start()
    stat_copy(NEAR, side_b).wait_recv()

    def early(c):
        receive(FAR, side_a, c)
        block_copy(BOTH, side_a, c).start()
        add_piece(FAR, side_a, c)
        receive(NEAR, side_b, c)
        add_piece(NEAR, side_b, c)

    for_pieces(early)

    for side in (side_a, side_b):
        stat_copy(BOTH, side).wait_recv()

    def late(c):
        receive(FAR, side_b, c)
        block_copy(BOTH, side_b, c).start()
        add_piece(FAR, side_b, c)
        receive(BOTH, side_b, c)
        add_piece(BOTH, side_b, c)

        @pl.when(c > 0)
        def _():
            receive(BOTH, side_a, c - 1)
            add_piece(BOTH, side_a, c - 1)

    for_pieces(late)

    def out_copies(side):
        return [
            pltpu.make_async_copy(total.at[index], ref, out_sem.at[index])
            for index, ref in ((0, image_grad_ref), (1, text_grad_ref))
        ]

    def finish(side):
        for start in range(0, rows, band):
            at = pl.ds(start, band)
            total[side, at, :] = scale * (
                total[side, at, :] - 2.0 * held[side, at, :].astype(jnp.float32)
            )
        for index, copy in enumerate(out_copies(side)):
            @pl.when(side == index)
            def _():
                copy.start()

    finish(side_b)
    receive(BOTH, side_a, pieces - 1)
    add_piece(BOTH, side_a, pieces - 1)
    finish(side_a)

    for kind in (NEAR, FAR, BOTH):
        for side in (side_a, side_b):
            stat_copy(kind, side).wait_send()

            def sent(c):
                block_copy(kind, side, c).wait_send()

            for_pieces(sent)
    for copy in out_copies(0):
        copy.wait()


def local(image_embeds, text_embeds, image_lse, text_lse, logit_scale):
    rows, width = image_embeds.shape
    piece = 128
    pieces = rows // piece
    dma = pltpu.SemaphoreType.DMA
    grad = jax.ShapeDtypeStruct((rows, width), jnp.float32)
    anywhere = pl.BlockSpec(memory_space=pl.ANY)
    return pl.pallas_call(
        functools.partial(kernel, piece),
        out_shape=(grad, grad),
        in_specs=[pl.BlockSpec(memory_space=pltpu.SMEM)] + [anywhere] * 4,
        out_specs=(anywhere, anywhere),
        scratch_shapes=[
            pltpu.VMEM((2, rows, width), jnp.bfloat16),
            pltpu.VMEM((2, 1, rows), jnp.float32),
            pltpu.VMEM((2, rows, LANES), jnp.float32),
            pltpu.VMEM((3, 2, rows, width), jnp.bfloat16),
            pltpu.VMEM((3, 2, 1, rows), jnp.float32),
            pltpu.VMEM((2, rows, width), jnp.float32),
            dma((4,)),
            dma((3, 2, pieces)),
            dma((3, 2, pieces)),
            dma((3, 2)),
            dma((3, 2)),
            dma((2,)),
        ],
        compiler_params=pltpu.CompilerParams(
            collective_id=0, has_side_effects=True, vmem_limit_bytes=32 * 1024 * 1024
        ),
        cost_estimate=pl.CostEstimate(
            flops=32 * rows * rows * width,
            bytes_accessed=12 * rows * width,
            transcendentals=16 * rows * rows,
        ),
    )(
        logit_scale.reshape(1, 1),
        image_embeds,
        text_embeds,
        image_lse.reshape(1, rows),
        text_lse.reshape(1, rows),
    )


def solution(mesh):
    return jax.shard_map(
        local,
        mesh=mesh,
        in_specs=(
            P(("outer", "inner"), None),
            P(("outer", "inner"), None),
            P(("outer", "inner")),
            P(("outer", "inner")),
            P(),
        ),
        out_specs=(P(("outer", "inner"), None), P(("outer", "inner"), None)),
        check_vma=False,
    )
```

```python
import functools
import math

import jax
import jax.numpy as jnp
from jax import lax
from jax.experimental import pallas as pl
from jax.experimental.pallas import tpu as pltpu
from jax.sharding import PartitionSpec as P

MESH = pl.DeviceIdType.MESH
LOG2E = math.log2(math.e)
LANES = 128
NEAR, FAR, BOTH = 0, 1, 2
NT = (((1,), (1,)), ((), ()))


def kernel(
    piece,
    scale_ref,
    images_ref,
    texts_ref,
    image_lse_ref,
    text_lse_ref,
    total,
    held,
    stat,
    column,
    got,
    got_stat,
    load_sem,
    send_sem,
    recv_sem,
    stat_send_sem,
    stat_recv_sem,
):
    rows, width = images_ref.shape
    band = 256
    pieces = rows // piece
    outer, inner = lax.axis_index("outer"), lax.axis_index("inner")
    n_outer, n_inner = lax.axis_size("outer"), lax.axis_size("inner")
    scale = scale_ref[0, 0]
    factor = scale * LOG2E

    loads = [
        pltpu.make_async_copy(source, target, load_sem.at[index])
        for index, (source, target) in enumerate(
            [
                (texts_ref, held.at[0]),
                (images_ref, held.at[1]),
                (text_lse_ref, stat.at[0]),
                (image_lse_ref, stat.at[1]),
            ]
        )
    ]
    for load in loads:
        load.start()

    barrier = pltpu.get_barrier_semaphore()
    for step in (1, -1):
        pl.semaphore_signal(
            barrier, inc=1, device_id={"outer": (outer + step + n_outer) % n_outer},
            device_id_type=MESH,
        )
        pl.semaphore_signal(
            barrier, inc=1, device_id={"inner": (inner + step + n_inner) % n_inner},
            device_id_type=MESH,
        )
    pl.semaphore_wait(barrier, 4)
    for load in loads:
        load.wait()

    side_a = 1 - inner % 2
    side_b = inner % 2

    def target(kind, side):
        step = 1 - 2 * side
        if kind == FAR:
            return {"outer": (outer + step + n_outer) % n_outer}
        return {"inner": (inner + step + n_inner) % n_inner}

    def span(c):
        return pl.ds(pl.multiple_of(c * piece, piece), piece)

    def block_copy(kind, side, c):
        source = got.at[FAR, side, span(c)] if kind == BOTH else held.at[side, span(c)]
        return pltpu.make_async_remote_copy(
            src_ref=source,
            dst_ref=got.at[kind, side, span(c)],
            send_sem=send_sem.at[kind, side, c],
            recv_sem=recv_sem.at[kind, side, c],
            device_id=target(kind, side),
            device_id_type=MESH,
        )

    def stat_copy(kind, side):
        source = got_stat.at[FAR, side] if kind == BOTH else stat.at[side]
        return pltpu.make_async_remote_copy(
            src_ref=source,
            dst_ref=got_stat.at[kind, side],
            send_sem=stat_send_sem.at[kind, side],
            recv_sem=stat_recv_sem.at[kind, side],
            device_id=target(kind, side),
            device_id_type=MESH,
        )

    def for_pieces(body):
        def step(c, carry):
            body(c)
            return carry

        lax.fori_loop(0, pieces, step, 0)

    for side in (side_a, side_b):
        for kind in (FAR, NEAR):
            stat_copy(kind, side).start()

    def send_first(c):
        block_copy(FAR, side_a, c).start()
        block_copy(NEAR, side_a, c).start()

    def send_near(c):
        block_copy(NEAR, side_b, c).start()

    for_pieces(send_first)
    for_pieces(send_near)

    for side in (0, 1):
        column[side] = jnp.broadcast_to(stat[side] * LOG2E, (LANES, rows)).T
    total[side_b] = jnp.zeros((rows, width), jnp.float32)

    def contribution(side, start, block, row):
        scores = factor * lax.dot_general(
            held[1 - side, pl.ds(start, band), :], block, NT,
            preferred_element_type=jnp.float32,
        )
        wide = jnp.concatenate(
            [column[1 - side, pl.ds(start, band), :]] * (block.shape[0] // LANES), axis=1
        )
        weights = (jnp.exp2(scores - wide) + jnp.exp2(scores - row)).astype(jnp.bfloat16)
        return jnp.dot(weights, block, preferred_element_type=jnp.float32)

    def own(side, at):
        return held[side, at, :], stat[side, :, at]

    def arrived(kind, side, at):
        return got[kind, side, at, :], got_stat[kind, side, :, at]

    def add(side, parts, fresh=False):
        block = jnp.concatenate([part[0] for part in parts], axis=0)
        row = jnp.concatenate([part[1] for part in parts], axis=1) * LOG2E
        for start in range(0, rows, band):
            term = contribution(side, start, block, row)
            if fresh:
                total[side, pl.ds(start, band), :] = term
            else:
                total[side, pl.ds(start, band), :] += term

    def receive(kind, side, c):
        block_copy(kind, side, c).wait_recv()

    half = rows // 2
    for index in range(2):
        add(side_a, [own(side_a, pl.ds(index * half, half))], fresh=index == 0)

    for side in (side_a, side_b):
        stat_copy(NEAR, side).wait_recv()
        stat_copy(FAR, side).wait_recv()
        stat_copy(BOTH, side).start()

    def early(c):
        at = span(c)
        receive(FAR, side_a, c)
        block_copy(BOTH, side_a, c).start()
        block_copy(FAR, side_a, c).wait_send()
        block_copy(FAR, side_b, c).start()
        receive(NEAR, side_a, c)
        add(side_a, [arrived(FAR, side_a, at), arrived(NEAR, side_a, at)])
        receive(NEAR, side_b, c)
        add(side_b, [own(side_b, at), arrived(NEAR, side_b, at)])

    for_pieces(early)

    for side in (side_a, side_b):
        stat_copy(BOTH, side).wait_recv()

    def last(index):
        for c in range(index * pieces // 2, (index + 1) * pieces // 2):
            receive(BOTH, side_a, c)
        add(side_a, [arrived(BOTH, side_a, pl.ds(index * half, half))])

    def late(c):
        at = span(c)
        receive(FAR, side_b, c)
        block_copy(BOTH, side_b, c).start()
        receive(BOTH, side_b, c)
        add(side_b, [arrived(FAR, side_b, at), arrived(BOTH, side_b, at)])

        @pl.when(c == pieces // 2)
        def _():
            last(0)

    for_pieces(late)
    last(1)

    for kind in (NEAR, FAR, BOTH):
        for side in (side_a, side_b):
            stat_copy(kind, side).wait_send()
            if kind == FAR and side is side_a:
                continue

            def sent(c):
                block_copy(kind, side, c).wait_send()

            for_pieces(sent)


def local(image_embeds, text_embeds, image_lse, text_lse, logit_scale):
    rows, width = image_embeds.shape
    piece = 128
    pieces = rows // piece
    dma = pltpu.SemaphoreType.DMA
    anywhere = pl.BlockSpec(memory_space=pltpu.HBM)
    total = pl.pallas_call(
        functools.partial(kernel, piece),
        out_shape=jax.ShapeDtypeStruct((2, rows, width), jnp.float32),
        in_specs=[pl.BlockSpec(memory_space=pltpu.SMEM)] + [anywhere] * 4,
        out_specs=pl.BlockSpec(memory_space=pltpu.VMEM),
        scratch_shapes=[
            pltpu.VMEM((2, rows, width), jnp.bfloat16),
            pltpu.VMEM((2, 1, rows), jnp.float32),
            pltpu.VMEM((2, rows, LANES), jnp.float32),
            pltpu.VMEM((3, 2, rows, width), jnp.bfloat16),
            pltpu.VMEM((3, 2, 1, rows), jnp.float32),
            dma((4,)),
            dma((3, 2, pieces)),
            dma((3, 2, pieces)),
            dma((3, 2)),
            dma((3, 2)),
        ],
        compiler_params=pltpu.CompilerParams(
            collective_id=0, has_side_effects=True, vmem_limit_bytes=60 * 1024 * 1024
        ),
        cost_estimate=pl.CostEstimate(
            flops=32 * rows * rows * width,
            bytes_accessed=12 * rows * width,
            transcendentals=16 * rows * rows,
        ),
    )(
        logit_scale.reshape(1, 1),
        image_embeds,
        text_embeds,
        image_lse.reshape(1, rows),
        text_lse.reshape(1, rows),
    )
    image_grad = logit_scale * (total[0] - 2.0 * text_embeds.astype(jnp.float32))
    text_grad = logit_scale * (total[1] - 2.0 * image_embeds.astype(jnp.float32))
    return image_grad, text_grad


def solution(mesh):
    return jax.shard_map(
        local,
        mesh=mesh,
        in_specs=(
            P(("outer", "inner"), None),
            P(("outer", "inner"), None),
            P(("outer", "inner")),
            P(("outer", "inner")),
            P(),
        ),
        out_specs=(P(("outer", "inner"), None), P(("outer", "inner"), None)),
        check_vma=False,
    )
```

```python
import functools
import math

import jax
import jax.numpy as jnp
from jax import lax
from jax.experimental import pallas as pl
from jax.experimental.pallas import tpu as pltpu
from jax.sharding import PartitionSpec as P

MESH = pl.DeviceIdType.MESH
LOG2E = math.log2(math.e)
LANES = 128
NEAR, FAR, BOTH = 0, 1, 2
NT = (((1,), (1,)), ((), ()))


def kernel(
    piece,
    scale_ref,
    images_ref,
    texts_ref,
    image_lse_ref,
    text_lse_ref,
    total,
    held,
    stat,
    column,
    got,
    got_stat,
    load_sem,
    send_sem,
    recv_sem,
    stat_send_sem,
    stat_recv_sem,
):
    rows, width = images_ref.shape
    band = 256
    pieces = rows // piece
    outer, inner = lax.axis_index("outer"), lax.axis_index("inner")
    n_outer, n_inner = lax.axis_size("outer"), lax.axis_size("inner")
    scale = scale_ref[0, 0]
    factor = scale * LOG2E

    loads = [
        pltpu.make_async_copy(source, target, load_sem.at[index])
        for index, (source, target) in enumerate(
            [
                (texts_ref, held.at[0]),
                (images_ref, held.at[1]),
                (text_lse_ref, stat.at[0]),
                (image_lse_ref, stat.at[1]),
            ]
        )
    ]
    for load in loads:
        load.start()

    barrier = pltpu.get_barrier_semaphore()
    for step in (1, -1):
        pl.semaphore_signal(
            barrier, inc=1, device_id={"outer": (outer + step + n_outer) % n_outer},
            device_id_type=MESH,
        )
        pl.semaphore_signal(
            barrier, inc=1, device_id={"inner": (inner + step + n_inner) % n_inner},
            device_id_type=MESH,
        )
    pl.semaphore_wait(barrier, 4)
    for load in loads:
        load.wait()

    side_a = 1 - inner % 2
    side_b = inner % 2

    def target(kind, side):
        step = 1 - 2 * side
        if kind == FAR:
            return {"outer": (outer + step + n_outer) % n_outer}
        return {"inner": (inner + step + n_inner) % n_inner}

    def span(c):
        return pl.ds(pl.multiple_of(c * piece, piece), piece)

    def block_copy(kind, side, c):
        source = got.at[FAR, side, span(c)] if kind == BOTH else held.at[side, span(c)]
        return pltpu.make_async_remote_copy(
            src_ref=source,
            dst_ref=got.at[kind, side, span(c)],
            send_sem=send_sem.at[kind, side, c],
            recv_sem=recv_sem.at[kind, side, c],
            device_id=target(kind, side),
            device_id_type=MESH,
        )

    def stat_copy(kind, side):
        source = got_stat.at[FAR, side] if kind == BOTH else stat.at[side]
        return pltpu.make_async_remote_copy(
            src_ref=source,
            dst_ref=got_stat.at[kind, side],
            send_sem=stat_send_sem.at[kind, side],
            recv_sem=stat_recv_sem.at[kind, side],
            device_id=target(kind, side),
            device_id_type=MESH,
        )

    def for_pieces(body):
        def step(c, carry):
            body(c)
            return carry

        lax.fori_loop(0, pieces, step, 0)

    for side in (side_a, side_b):
        for kind in (FAR, NEAR):
            stat_copy(kind, side).start()

    def send_first(c):
        block_copy(FAR, side_a, c).start()
        block_copy(NEAR, side_a, c).start()

    def send_near(c):
        block_copy(NEAR, side_b, c).start()

    for_pieces(send_first)
    for_pieces(send_near)

    for side in (0, 1):
        column[side] = jnp.broadcast_to(stat[side] * LOG2E, (LANES, rows)).T
    total[side_b] = jnp.zeros((rows, width), jnp.float32)

    def contribution(side, start, block, row):
        scores = factor * lax.dot_general(
            held[1 - side, pl.ds(start, band), :], block, NT,
            preferred_element_type=jnp.float32,
        )
        wide = jnp.concatenate(
            [column[1 - side, pl.ds(start, band), :]] * (block.shape[0] // LANES), axis=1
        )
        weights = (jnp.exp2(scores - wide) + jnp.exp2(scores - row)).astype(jnp.bfloat16)
        return jnp.dot(weights, block, preferred_element_type=jnp.float32)

    def own(side, at):
        return held[side, at, :], stat[side, :, at]

    def arrived(kind, side, at):
        return got[kind, side, at, :], got_stat[kind, side, :, at]

    def add(side, parts, fresh=False):
        block = jnp.concatenate([part[0] for part in parts], axis=0)
        row = jnp.concatenate([part[1] for part in parts], axis=1) * LOG2E
        for start in range(0, rows, band):
            term = contribution(side, start, block, row)
            if fresh:
                total[side, pl.ds(start, band), :] = term
            else:
                total[side, pl.ds(start, band), :] += term

    def receive(kind, side, c):
        block_copy(kind, side, c).wait_recv()

    half = rows // 2
    for index in range(2):
        add(side_a, [own(side_a, pl.ds(index * half, half))], fresh=index == 0)

    for side in (side_a, side_b):
        stat_copy(NEAR, side).wait_recv()
        stat_copy(FAR, side).wait_recv()
        stat_copy(BOTH, side).start()

    def early(c):
        at = span(c)
        block_copy(FAR, side_a, c).wait_send()
        block_copy(FAR, side_b, c).start()
        receive(FAR, side_a, c)
        block_copy(BOTH, side_a, c).start()
        receive(NEAR, side_a, c)
        add(side_a, [arrived(FAR, side_a, at), arrived(NEAR, side_a, at)])
        receive(NEAR, side_b, c)
        add(side_b, [own(side_b, at), arrived(NEAR, side_b, at)])

    for_pieces(early)

    for side in (side_a, side_b):
        stat_copy(BOTH, side).wait_recv()

    def last(index):
        for c in range(index * pieces // 2, (index + 1) * pieces // 2):
            receive(BOTH, side_a, c)
        add(side_a, [arrived(BOTH, side_a, pl.ds(index * half, half))])

    def late(c):
        at = span(c)
        receive(FAR, side_b, c)
        block_copy(BOTH, side_b, c).start()
        receive(BOTH, side_b, c)
        add(side_b, [arrived(FAR, side_b, at), arrived(BOTH, side_b, at)])

        @pl.when(c == pieces // 2)
        def _():
            last(0)

    for_pieces(late)
    last(1)

    for kind in (NEAR, FAR, BOTH):
        for side in (side_a, side_b):
            stat_copy(kind, side).wait_send()
            if kind == FAR and side is side_a:
                continue

            def sent(c):
                block_copy(kind, side, c).wait_send()

            for_pieces(sent)


def local(image_embeds, text_embeds, image_lse, text_lse, logit_scale):
    rows, width = image_embeds.shape
    piece = 128
    pieces = rows // piece
    dma = pltpu.SemaphoreType.DMA
    anywhere = pl.BlockSpec(memory_space=pltpu.HBM)
    total = pl.pallas_call(
        functools.partial(kernel, piece),
        out_shape=jax.ShapeDtypeStruct((2, rows, width), jnp.float32),
        in_specs=[pl.BlockSpec(memory_space=pltpu.SMEM)] + [anywhere] * 4,
        out_specs=pl.BlockSpec(memory_space=pltpu.VMEM),
        scratch_shapes=[
            pltpu.VMEM((2, rows, width), jnp.bfloat16),
            pltpu.VMEM((2, 1, rows), jnp.float32),
            pltpu.VMEM((2, rows, LANES), jnp.float32),
            pltpu.VMEM((3, 2, rows, width), jnp.bfloat16),
            pltpu.VMEM((3, 2, 1, rows), jnp.float32),
            dma((4,)),
            dma((3, 2, pieces)),
            dma((3, 2, pieces)),
            dma((3, 2)),
            dma((3, 2)),
        ],
        compiler_params=pltpu.CompilerParams(
            collective_id=0, has_side_effects=True, vmem_limit_bytes=60 * 1024 * 1024
        ),
        cost_estimate=pl.CostEstimate(
            flops=32 * rows * rows * width,
            bytes_accessed=12 * rows * width,
            transcendentals=16 * rows * rows,
        ),
    )(
        logit_scale.reshape(1, 1),
        image_embeds,
        text_embeds,
        image_lse.reshape(1, rows),
        text_lse.reshape(1, rows),
    )
    image_grad = logit_scale * (total[0] - 2.0 * text_embeds.astype(jnp.float32))
    text_grad = logit_scale * (total[1] - 2.0 * image_embeds.astype(jnp.float32))
    return image_grad, text_grad


def solution(mesh):
    return jax.shard_map(
        local,
        mesh=mesh,
        in_specs=(
            P(("outer", "inner"), None),
            P(("outer", "inner"), None),
            P(("outer", "inner")),
            P(("outer", "inner")),
            P(),
        ),
        out_specs=(P(("outer", "inner"), None), P(("outer", "inner"), None)),
        check_vma=False,
    )
```

```python
import functools
import math

import jax
import jax.numpy as jnp
from jax import lax
from jax.experimental import pallas as pl
from jax.experimental.pallas import tpu as pltpu
from jax.sharding import PartitionSpec as P

MESH = pl.DeviceIdType.MESH
LOG2E = math.log2(math.e)
LANES = 128
NEAR, FAR, BOTH = 0, 1, 2
NT = (((1,), (1,)), ((), ()))


def kernel(
    piece,
    scale_ref,
    images_ref,
    texts_ref,
    image_lse_ref,
    text_lse_ref,
    total,
    held,
    stat,
    column,
    got,
    got_stat,
    load_sem,
    send_sem,
    recv_sem,
    stat_send_sem,
    stat_recv_sem,
):
    rows, width = images_ref.shape
    band = 256
    pieces = rows // piece
    outer, inner = lax.axis_index("outer"), lax.axis_index("inner")
    n_outer, n_inner = lax.axis_size("outer"), lax.axis_size("inner")
    scale = scale_ref[0, 0]
    factor = scale * LOG2E

    loads = [
        pltpu.make_async_copy(source, target, load_sem.at[index])
        for index, (source, target) in enumerate(
            [
                (texts_ref, held.at[0]),
                (images_ref, held.at[1]),
                (text_lse_ref, stat.at[0]),
                (image_lse_ref, stat.at[1]),
            ]
        )
    ]
    for load in loads:
        load.start()

    barrier = pltpu.get_barrier_semaphore()
    for step in (1, -1):
        pl.semaphore_signal(
            barrier, inc=1, device_id={"outer": (outer + step + n_outer) % n_outer},
            device_id_type=MESH,
        )
        pl.semaphore_signal(
            barrier, inc=1, device_id={"inner": (inner + step + n_inner) % n_inner},
            device_id_type=MESH,
        )
    pl.semaphore_wait(barrier, 4)
    for load in loads:
        load.wait()

    side_a = 1 - inner % 2
    side_b = inner % 2

    def target(kind, side):
        step = 1 - 2 * side
        if kind == FAR:
            return {"outer": (outer + step + n_outer) % n_outer}
        return {"inner": (inner + step + n_inner) % n_inner}

    def span(c):
        return pl.ds(pl.multiple_of(c * piece, piece), piece)

    def block_copy(kind, side, c):
        source = got.at[FAR, side, span(c)] if kind == BOTH else held.at[side, span(c)]
        return pltpu.make_async_remote_copy(
            src_ref=source,
            dst_ref=got.at[kind, side, span(c)],
            send_sem=send_sem.at[kind, side, c],
            recv_sem=recv_sem.at[kind, side, c],
            device_id=target(kind, side),
            device_id_type=MESH,
        )

    def stat_copy(kind, side):
        source = got_stat.at[FAR, side] if kind == BOTH else stat.at[side]
        return pltpu.make_async_remote_copy(
            src_ref=source,
            dst_ref=got_stat.at[kind, side],
            send_sem=stat_send_sem.at[kind, side],
            recv_sem=stat_recv_sem.at[kind, side],
            device_id=target(kind, side),
            device_id_type=MESH,
        )

    def for_pieces(body):
        def step(c, carry):
            body(c)
            return carry

        lax.fori_loop(0, pieces, step, 0)

    for side in (side_a, side_b):
        for kind in (FAR, NEAR):
            stat_copy(kind, side).start()

    ahead = 2

    def send_far(m):
        late_side = m // pieces
        block_copy(FAR, side_a + late_side * (side_b - side_a), m % pieces).start()

    def send_near(c):
        block_copy(NEAR, side_b, c).start()

    for c in range(ahead):
        send_far(c)
        block_copy(NEAR, side_a, c).start()
    for_pieces(send_near)

    for side in (0, 1):
        column[side] = jnp.broadcast_to(stat[side] * LOG2E, (LANES, rows)).T
    total[side_b] = jnp.zeros((rows, width), jnp.float32)

    def contribution(side, start, block, row):
        scores = factor * lax.dot_general(
            held[1 - side, pl.ds(start, band), :], block, NT,
            preferred_element_type=jnp.float32,
        )
        wide = jnp.concatenate(
            [column[1 - side, pl.ds(start, band), :]] * (block.shape[0] // LANES), axis=1
        )
        weights = (jnp.exp2(scores - wide) + jnp.exp2(scores - row)).astype(jnp.bfloat16)
        return jnp.dot(weights, block, preferred_element_type=jnp.float32)

    def own(side, at):
        return held[side, at, :], stat[side, :, at]

    def arrived(kind, side, at):
        return got[kind, side, at, :], got_stat[kind, side, :, at]

    def add(side, parts, fresh=False):
        block = jnp.concatenate([part[0] for part in parts], axis=0)
        row = jnp.concatenate([part[1] for part in parts], axis=1) * LOG2E
        for start in range(0, rows, band):
            term = contribution(side, start, block, row)
            if fresh:
                total[side, pl.ds(start, band), :] = term
            else:
                total[side, pl.ds(start, band), :] += term

    def receive(kind, side, c):
        block_copy(kind, side, c).wait_recv()

    half = rows // 2
    for index in range(2):
        add(side_a, [own(side_a, pl.ds(index * half, half))], fresh=index == 0)

    for side in (side_a, side_b):
        stat_copy(NEAR, side).wait_recv()
        stat_copy(FAR, side).wait_recv()
        stat_copy(BOTH, side).start()

    def early(c):
        at = span(c)
        block_copy(FAR, side_a, c).wait_send()
        send_far(c + ahead)
        receive(FAR, side_a, c)
        block_copy(NEAR, side_a, c).wait_send()

        @pl.when(c < pieces - ahead)
        def _():
            block_copy(NEAR, side_a, c + ahead).start()

        @pl.when(c >= pieces - ahead)
        def _():
            block_copy(BOTH, side_a, c + ahead - pieces).start()

        receive(NEAR, side_a, c)
        add(side_a, [arrived(FAR, side_a, at), arrived(NEAR, side_a, at)])
        receive(NEAR, side_b, c)
        add(side_b, [own(side_b, at), arrived(NEAR, side_b, at)])

    for_pieces(early)

    for side in (side_a, side_b):
        stat_copy(BOTH, side).wait_recv()

    def last(index):
        for c in range(index * pieces // 2, (index + 1) * pieces // 2):
            receive(BOTH, side_a, c)
        add(side_a, [arrived(BOTH, side_a, pl.ds(index * half, half))])

    def late(c):
        at = span(c)
        block_copy(FAR, side_b, c).wait_send()
        block_copy(BOTH, side_a, c).wait_send()

        @pl.when(c < pieces - ahead)
        def _():
            send_far(c + ahead + pieces)
            block_copy(BOTH, side_a, c + ahead).start()

        receive(FAR, side_b, c)
        block_copy(BOTH, side_b, c).start()
        receive(BOTH, side_b, c)
        add(side_b, [arrived(FAR, side_b, at), arrived(BOTH, side_b, at)])

        @pl.when(c == pieces // 2)
        def _():
            last(0)

    for_pieces(late)
    last(1)

    for kind in (NEAR, FAR, BOTH):
        for side in (side_a, side_b):
            stat_copy(kind, side).wait_send()
    for kind in (NEAR, BOTH):

        def sent(c):
            block_copy(kind, side_b, c).wait_send()

        for_pieces(sent)


def local(image_embeds, text_embeds, image_lse, text_lse, logit_scale):
    rows, width = image_embeds.shape
    piece = 128
    pieces = rows // piece
    dma = pltpu.SemaphoreType.DMA
    anywhere = pl.BlockSpec(memory_space=pltpu.HBM)
    total = pl.pallas_call(
        functools.partial(kernel, piece),
        out_shape=pltpu.VMEM((2, rows, width), jnp.float32),
        in_specs=[pl.BlockSpec(memory_space=pltpu.SMEM)] + [anywhere] * 4,
        out_specs=pl.BlockSpec(memory_space=pltpu.VMEM),
        scratch_shapes=[
            pltpu.VMEM((2, rows, width), jnp.bfloat16),
            pltpu.VMEM((2, 1, rows), jnp.float32),
            pltpu.VMEM((2, rows, LANES), jnp.float32),
            pltpu.VMEM((3, 2, rows, width), jnp.bfloat16),
            pltpu.VMEM((3, 2, 1, rows), jnp.float32),
            dma((4,)),
            dma((3, 2, pieces)),
            dma((3, 2, pieces)),
            dma((3, 2)),
            dma((3, 2)),
        ],
        compiler_params=pltpu.CompilerParams(
            collective_id=0, has_side_effects=True, vmem_limit_bytes=60 * 1024 * 1024
        ),
        cost_estimate=pl.CostEstimate(
            flops=32 * rows * rows * width,
            bytes_accessed=12 * rows * width,
            transcendentals=16 * rows * rows,
        ),
    )(
        logit_scale.reshape(1, 1),
        image_embeds,
        text_embeds,
        image_lse.reshape(1, rows),
        text_lse.reshape(1, rows),
    )
    image_grad = logit_scale * (total[0] - 2.0 * text_embeds.astype(jnp.float32))
    text_grad = logit_scale * (total[1] - 2.0 * image_embeds.astype(jnp.float32))
    return image_grad, text_grad


def solution(mesh):
    return jax.shard_map(
        local,
        mesh=mesh,
        in_specs=(
            P(("outer", "inner"), None),
            P(("outer", "inner"), None),
            P(("outer", "inner")),
            P(("outer", "inner")),
            P(),
        ),
        out_specs=(P(("outer", "inner"), None), P(("outer", "inner"), None)),
        check_vma=False,
    )
```

```python
import functools
import math

import jax
import jax.numpy as jnp
from jax import lax
from jax.experimental import pallas as pl
from jax.experimental.pallas import tpu as pltpu
from jax.sharding import PartitionSpec as P

MESH = pl.DeviceIdType.MESH
LOG2E = math.log2(math.e)
LANES = 128
NEAR, FAR, BOTH = 0, 1, 2
NT = (((1,), (1,)), ((), ()))


def kernel(
    piece,
    scale_ref,
    images_ref,
    texts_ref,
    image_lse_ref,
    text_lse_ref,
    total,
    held,
    stat,
    column,
    got,
    got_stat,
    load_sem,
    send_sem,
    recv_sem,
    stat_send_sem,
    stat_recv_sem,
    ready_sem,
):
    rows, width = images_ref.shape
    band = 256
    pieces = rows // piece
    outer, inner = lax.axis_index("outer"), lax.axis_index("inner")
    n_outer, n_inner = lax.axis_size("outer"), lax.axis_size("inner")
    scale = scale_ref[0, 0]
    factor = scale * LOG2E

    loads = [
        pltpu.make_async_copy(source, target, load_sem.at[index])
        for index, (source, target) in enumerate(
            [
                (texts_ref, held.at[0]),
                (images_ref, held.at[1]),
                (text_lse_ref, stat.at[0]),
                (image_lse_ref, stat.at[1]),
            ]
        )
    ]
    for load in loads:
        load.start()

    first, last_group = outer == 0, outer == n_outer - 1
    barrier = pltpu.get_barrier_semaphore()
    for step in (1, -1):
        pl.semaphore_signal(
            barrier, inc=1, device_id={"inner": (inner + step + n_inner) % n_inner},
            device_id_type=MESH,
        )
    pl.semaphore_signal(
        barrier, inc=1, device_id={"outer": (outer - 1 + n_outer) % n_outer},
        device_id_type=MESH,
    )

    @pl.when(jnp.logical_not(last_group))
    def _():
        pl.semaphore_signal(
            barrier, inc=1, device_id={"outer": (outer + 1) % n_outer}, device_id_type=MESH
        )

    @pl.when(first)
    def _():
        pl.semaphore_wait(barrier, 3)

    @pl.when(jnp.logical_not(first))
    def _():
        pl.semaphore_wait(barrier, 4)

    @pl.when(last_group)
    def _():
        pl.semaphore_signal(
            ready_sem, inc=1, device_id={"outer": (outer + 1) % n_outer}, device_id_type=MESH
        )

    for load in loads:
        load.wait()

    side_a = 1 - inner % 2
    side_b = inner % 2
    wait_soon = jnp.logical_and(first, side_a == 1)
    wait_later = jnp.logical_and(first, side_a == 0)

    def target(kind, side):
        step = 1 - 2 * side
        if kind == FAR:
            return {"outer": (outer + step + n_outer) % n_outer}
        return {"inner": (inner + step + n_inner) % n_inner}

    def span(c):
        return pl.ds(pl.multiple_of(c * piece, piece), piece)

    def block_copy(kind, side, c):
        source = got.at[FAR, side, span(c)] if kind == BOTH else held.at[side, span(c)]
        return pltpu.make_async_remote_copy(
            src_ref=source,
            dst_ref=got.at[kind, side, span(c)],
            send_sem=send_sem.at[kind, side, c],
            recv_sem=recv_sem.at[kind, side, c],
            device_id=target(kind, side),
            device_id_type=MESH,
        )

    def stat_copy(kind, side):
        source = got_stat.at[FAR, side] if kind == BOTH else stat.at[side]
        return pltpu.make_async_remote_copy(
            src_ref=source,
            dst_ref=got_stat.at[kind, side],
            send_sem=stat_send_sem.at[kind, side],
            recv_sem=stat_recv_sem.at[kind, side],
            device_id=target(kind, side),
            device_id_type=MESH,
        )

    def for_pieces(body):
        def step(c, carry):
            body(c)
            return carry

        lax.fori_loop(0, pieces, step, 0)

    stat_copy(FAR, 0).start()
    for side in (0, 1):
        stat_copy(NEAR, side).start()

    ahead = 2

    def send_far(m):
        late_side = m // pieces
        block_copy(FAR, side_a + late_side * (side_b - side_a), m % pieces).start()

    def send_near(c):
        block_copy(NEAR, side_b, c).start()

    def open_far():
        for c in range(ahead):
            send_far(c)

    pl.when(jnp.logical_not(wait_soon))(open_far)
    for c in range(ahead):
        block_copy(NEAR, side_a, c).start()
    for_pieces(send_near)

    for side in (0, 1):
        column[side] = jnp.broadcast_to(stat[side] * LOG2E, (LANES, rows)).T
    total[side_b] = jnp.zeros((rows, width), jnp.float32)

    def contribution(side, start, block, row):
        scores = factor * lax.dot_general(
            held[1 - side, pl.ds(start, band), :], block, NT,
            preferred_element_type=jnp.float32,
        )
        wide = jnp.concatenate(
            [column[1 - side, pl.ds(start, band), :]] * (block.shape[0] // LANES), axis=1
        )
        weights = (jnp.exp2(scores - wide) + jnp.exp2(scores - row)).astype(jnp.bfloat16)
        return jnp.dot(weights, block, preferred_element_type=jnp.float32)

    def own(side, at):
        return held[side, at, :], stat[side, :, at]

    def arrived(kind, side, at):
        return got[kind, side, at, :], got_stat[kind, side, :, at]

    def add(side, parts, fresh=False):
        block = jnp.concatenate([part[0] for part in parts], axis=0)
        row = jnp.concatenate([part[1] for part in parts], axis=1) * LOG2E
        for start in range(0, rows, band):
            term = contribution(side, start, block, row)
            if fresh:
                total[side, pl.ds(start, band), :] = term
            else:
                total[side, pl.ds(start, band), :] += term

    def receive(kind, side, c):
        block_copy(kind, side, c).wait_recv()

    half = rows // 2
    for index in range(2):
        add(side_a, [own(side_a, pl.ds(index * half, half))], fresh=index == 0)

    @pl.when(wait_soon)
    def _():
        pl.semaphore_wait(ready_sem, 1)
        open_far()

    @pl.when(jnp.logical_not(wait_later))
    def _():
        stat_copy(FAR, 1).start()

    for side in (side_a, side_b):
        stat_copy(NEAR, side).wait_recv()
    stat_copy(FAR, side_a).wait_recv()
    stat_copy(BOTH, side_a).start()

    def early(c):
        at = span(c)
        block_copy(FAR, side_a, c).wait_send()

        @pl.when(jnp.logical_and(wait_later, c == pieces - ahead))
        def _():
            pl.semaphore_wait(ready_sem, 1)
            stat_copy(FAR, 1).start()

        send_far(c + ahead)
        receive(FAR, side_a, c)
        block_copy(NEAR, side_a, c).wait_send()

        @pl.when(c < pieces - ahead)
        def _():
            block_copy(NEAR, side_a, c + ahead).start()

        @pl.when(c >= pieces - ahead)
        def _():
            block_copy(BOTH, side_a, c + ahead - pieces).start()

        receive(NEAR, side_a, c)
        add(side_a, [arrived(FAR, side_a, at), arrived(NEAR, side_a, at)])
        receive(NEAR, side_b, c)
        add(side_b, [own(side_b, at), arrived(NEAR, side_b, at)])

    for_pieces(early)

    stat_copy(BOTH, side_b).wait_recv()

    def late(c):
        at = span(c)
        block_copy(FAR, side_b, c).wait_send()
        block_copy(BOTH, side_a, c).wait_send()

        @pl.when(c < pieces - ahead)
        def _():
            send_far(c + ahead + pieces)
            block_copy(BOTH, side_a, c + ahead).start()

        receive(FAR, side_b, c)
        block_copy(BOTH, side_b, c).start()

        @pl.when(c == 0)
        def _():
            stat_copy(FAR, side_b).wait_recv()
            stat_copy(BOTH, side_b).start()

        receive(BOTH, side_b, c)
        add(side_b, [arrived(FAR, side_b, at), arrived(BOTH, side_b, at)])

        @pl.when(c == pieces // 2)
        def _():
            stat_copy(BOTH, side_a).wait_recv()
            for index in range(pieces // 2):
                receive(BOTH, side_a, index)
            add(side_a, [arrived(BOTH, side_a, pl.ds(0, half))])

        @pl.when(c > pieces // 2)
        def _():
            receive(BOTH, side_a, c - 1)
            add(side_a, [arrived(BOTH, side_a, span(c - 1))])

    for_pieces(late)
    receive(BOTH, side_a, pieces - 1)
    add(side_a, [arrived(BOTH, side_a, span(pieces - 1))])

    for kind in (NEAR, FAR, BOTH):
        for side in (side_a, side_b):
            stat_copy(kind, side).wait_send()
    for kind in (NEAR, BOTH):

        def sent(c):
            block_copy(kind, side_b, c).wait_send()

        for_pieces(sent)


def local(image_embeds, text_embeds, image_lse, text_lse, logit_scale):
    rows, width = image_embeds.shape
    piece = 128
    pieces = rows // piece
    dma = pltpu.SemaphoreType.DMA
    anywhere = pl.BlockSpec(memory_space=pltpu.HBM)
    total = pl.pallas_call(
        functools.partial(kernel, piece),
        out_shape=pltpu.VMEM((2, rows, width), jnp.float32),
        in_specs=[pl.BlockSpec(memory_space=pltpu.SMEM)] + [anywhere] * 4,
        out_specs=pl.BlockSpec(memory_space=pltpu.VMEM),
        scratch_shapes=[
            pltpu.VMEM((2, rows, width), jnp.bfloat16),
            pltpu.VMEM((2, 1, rows), jnp.float32),
            pltpu.VMEM((2, rows, LANES), jnp.float32),
            pltpu.VMEM((3, 2, rows, width), jnp.bfloat16),
            pltpu.VMEM((3, 2, 1, rows), jnp.float32),
            dma((4,)),
            dma((3, 2, pieces)),
            dma((3, 2, pieces)),
            dma((3, 2)),
            dma((3, 2)),
            pltpu.SemaphoreType.REGULAR,
        ],
        compiler_params=pltpu.CompilerParams(
            collective_id=0, has_side_effects=True, vmem_limit_bytes=60 * 1024 * 1024
        ),
        cost_estimate=pl.CostEstimate(
            flops=32 * rows * rows * width,
            bytes_accessed=12 * rows * width,
            transcendentals=16 * rows * rows,
        ),
    )(
        logit_scale.reshape(1, 1),
        image_embeds,
        text_embeds,
        image_lse.reshape(1, rows),
        text_lse.reshape(1, rows),
    )
    image_grad = logit_scale * (total[0] - 2.0 * text_embeds.astype(jnp.float32))
    text_grad = logit_scale * (total[1] - 2.0 * image_embeds.astype(jnp.float32))
    return image_grad, text_grad


def solution(mesh):
    return jax.shard_map(
        local,
        mesh=mesh,
        in_specs=(
            P(("outer", "inner"), None),
            P(("outer", "inner"), None),
            P(("outer", "inner")),
            P(("outer", "inner")),
            P(),
        ),
        out_specs=(P(("outer", "inner"), None), P(("outer", "inner"), None)),
        check_vma=False,
    )
```

```python
import functools
import math

import jax
import jax.numpy as jnp
from jax import lax
from jax.experimental import pallas as pl
from jax.experimental.pallas import tpu as pltpu
from jax.sharding import PartitionSpec as P

MESH = pl.DeviceIdType.MESH
LOG2E = math.log2(math.e)
LANES = 128
NEAR, FAR, BOTH = 0, 1, 2
NT = (((1,), (1,)), ((), ()))


def kernel(
    piece,
    scale_ref,
    images_ref,
    texts_ref,
    image_lse_ref,
    text_lse_ref,
    total,
    held,
    stat,
    column,
    got,
    got_stat,
    load_sem,
    send_sem,
    recv_sem,
    stat_send_sem,
    stat_recv_sem,
    ready_sem,
):
    rows, width = images_ref.shape
    band = 256
    pieces = rows // piece
    outer, inner = lax.axis_index("outer"), lax.axis_index("inner")
    n_outer, n_inner = lax.axis_size("outer"), lax.axis_size("inner")
    scale = scale_ref[0, 0]
    factor = scale * LOG2E

    loads = [
        pltpu.make_async_copy(source, target, load_sem.at[index])
        for index, (source, target) in enumerate(
            [
                (texts_ref, held.at[0]),
                (images_ref, held.at[1]),
                (text_lse_ref, stat.at[0]),
                (image_lse_ref, stat.at[1]),
            ]
        )
    ]
    for load in loads:
        load.start()

    first, last_group = outer == 0, outer == n_outer - 1
    barrier = pltpu.get_barrier_semaphore()
    for step in (1, -1):
        pl.semaphore_signal(
            barrier, inc=1, device_id={"inner": (inner + step + n_inner) % n_inner},
            device_id_type=MESH,
        )
    pl.semaphore_signal(
        barrier, inc=1, device_id={"outer": (outer - 1 + n_outer) % n_outer},
        device_id_type=MESH,
    )

    @pl.when(jnp.logical_not(last_group))
    def _():
        pl.semaphore_signal(
            barrier, inc=1, device_id={"outer": (outer + 1) % n_outer}, device_id_type=MESH
        )

    @pl.when(first)
    def _():
        pl.semaphore_wait(barrier, 3)

    @pl.when(jnp.logical_not(first))
    def _():
        pl.semaphore_wait(barrier, 4)

    @pl.when(last_group)
    def _():
        pl.semaphore_signal(
            ready_sem, inc=1, device_id={"outer": (outer + 1) % n_outer}, device_id_type=MESH
        )

    for load in loads:
        load.wait()

    side_a, side_b = 0, 1

    def target(kind, side):
        step = 1 - 2 * side
        if kind == FAR:
            return {"outer": (outer + step + n_outer) % n_outer}
        return {"inner": (inner + step + n_inner) % n_inner}

    def span(c):
        return pl.ds(pl.multiple_of(c * piece, piece), piece)

    def block_copy(kind, side, c):
        source = got.at[FAR, side, span(c)] if kind == BOTH else held.at[side, span(c)]
        return pltpu.make_async_remote_copy(
            src_ref=source,
            dst_ref=got.at[kind, side, span(c)],
            send_sem=send_sem.at[kind, side, c],
            recv_sem=recv_sem.at[kind, side, c],
            device_id=target(kind, side),
            device_id_type=MESH,
        )

    def stat_copy(kind, side):
        source = got_stat.at[FAR, side] if kind == BOTH else stat.at[side]
        return pltpu.make_async_remote_copy(
            src_ref=source,
            dst_ref=got_stat.at[kind, side],
            send_sem=stat_send_sem.at[kind, side],
            recv_sem=stat_recv_sem.at[kind, side],
            device_id=target(kind, side),
            device_id_type=MESH,
        )

    def for_pieces(body):
        def step(c, carry):
            body(c)
            return carry

        lax.fori_loop(0, pieces, step, 0)

    stat_copy(FAR, 0).start()
    for side in (0, 1):
        stat_copy(NEAR, side).start()

    ahead = 2

    def send_far(m):
        late_side = m // pieces
        block_copy(FAR, side_a + late_side * (side_b - side_a), m % pieces).start()

    def send_near(c):
        block_copy(NEAR, side_b, c).start()

    def open_far():
        for c in range(ahead):
            send_far(c)

    open_far()
    for c in range(ahead):
        block_copy(NEAR, side_a, c).start()
    for_pieces(send_near)

    for side in (0, 1):
        column[side] = jnp.broadcast_to(stat[side] * LOG2E, (LANES, rows)).T
    total[side_b] = jnp.zeros((rows, width), jnp.float32)

    def contribution(side, start, block, row):
        scores = factor * lax.dot_general(
            held[1 - side, pl.ds(start, band), :], block, NT,
            preferred_element_type=jnp.float32,
        )
        wide = jnp.concatenate(
            [column[1 - side, pl.ds(start, band), :]] * (block.shape[0] // LANES), axis=1
        )
        weights = (jnp.exp2(scores - wide) + jnp.exp2(scores - row)).astype(jnp.bfloat16)
        return jnp.dot(weights, block, preferred_element_type=jnp.float32)

    def own(side, at):
        return held[side, at, :], stat[side, :, at]

    def arrived(kind, side, at):
        return got[kind, side, at, :], got_stat[kind, side, :, at]

    def add(side, parts, fresh=False):
        block = jnp.concatenate([part[0] for part in parts], axis=0)
        row = jnp.concatenate([part[1] for part in parts], axis=1) * LOG2E
        for start in range(0, rows, band):
            term = contribution(side, start, block, row)
            if fresh:
                total[side, pl.ds(start, band), :] = term
            else:
                total[side, pl.ds(start, band), :] += term

    def receive(kind, side, c):
        block_copy(kind, side, c).wait_recv()

    half = rows // 2
    for index in range(2):
        add(side_a, [own(side_a, pl.ds(index * half, half))], fresh=index == 0)

    @pl.when(jnp.logical_not(first))
    def _():
        stat_copy(FAR, 1).start()

    for side in (side_a, side_b):
        stat_copy(NEAR, side).wait_recv()
    stat_copy(FAR, side_a).wait_recv()
    stat_copy(BOTH, side_a).start()

    def early(c):
        at = span(c)
        block_copy(FAR, side_a, c).wait_send()

        @pl.when(jnp.logical_and(first, c == pieces - ahead))
        def _():
            pl.semaphore_wait(ready_sem, 1)
            stat_copy(FAR, 1).start()

        send_far(c + ahead)
        receive(FAR, side_a, c)
        block_copy(NEAR, side_a, c).wait_send()

        @pl.when(c < pieces - ahead)
        def _():
            block_copy(NEAR, side_a, c + ahead).start()

        @pl.when(c >= pieces - ahead)
        def _():
            block_copy(BOTH, side_a, c + ahead - pieces).start()

        receive(NEAR, side_a, c)
        add(side_a, [arrived(FAR, side_a, at), arrived(NEAR, side_a, at)])
        receive(NEAR, side_b, c)
        add(side_b, [own(side_b, at), arrived(NEAR, side_b, at)])

    for_pieces(early)

    stat_copy(BOTH, side_a).wait_recv()

    def forwarded(index):
        for c in range(index * pieces // 2, (index + 1) * pieces // 2):
            receive(BOTH, side_a, c)
        add(side_a, [arrived(BOTH, side_a, pl.ds(index * half, half))])

    def late(c):
        at = span(c)
        block_copy(FAR, side_b, c).wait_send()
        block_copy(BOTH, side_a, c).wait_send()

        @pl.when(c < pieces - ahead)
        def _():
            send_far(c + ahead + pieces)
            block_copy(BOTH, side_a, c + ahead).start()

        @pl.when(c == pieces // 2)
        def _():
            forwarded(0)

        @pl.when(c == pieces - 1)
        def _():
            forwarded(1)

        receive(FAR, side_b, c)
        block_copy(BOTH, side_b, c).start()

        @pl.when(c == 0)
        def _():
            stat_copy(FAR, side_b).wait_recv()
            stat_copy(BOTH, side_b).start()
            add(side_b, [arrived(FAR, side_b, at)])

        @pl.when(c == 1)
        def _():
            stat_copy(BOTH, side_b).wait_recv()

        @pl.when(c > 0)
        def _():
            receive(BOTH, side_b, c - 1)
            add(
                side_b,
                [arrived(FAR, side_b, at), arrived(BOTH, side_b, span(c - 1))],
            )

    for_pieces(late)
    receive(BOTH, side_b, pieces - 1)
    add(side_b, [arrived(BOTH, side_b, span(pieces - 1))])

    for kind in (NEAR, FAR, BOTH):
        for side in (side_a, side_b):
            stat_copy(kind, side).wait_send()
    for kind in (NEAR, BOTH):

        def sent(c):
            block_copy(kind, side_b, c).wait_send()

        for_pieces(sent)


def local(image_embeds, text_embeds, image_lse, text_lse, logit_scale):
    rows, width = image_embeds.shape
    piece = 128
    pieces = rows // piece
    dma = pltpu.SemaphoreType.DMA
    anywhere = pl.BlockSpec(memory_space=pltpu.HBM)
    total = pl.pallas_call(
        functools.partial(kernel, piece),
        out_shape=pltpu.VMEM((2, rows, width), jnp.float32),
        in_specs=[pl.BlockSpec(memory_space=pltpu.SMEM)] + [anywhere] * 4,
        out_specs=pl.BlockSpec(memory_space=pltpu.VMEM),
        scratch_shapes=[
            pltpu.VMEM((2, rows, width), jnp.bfloat16),
            pltpu.VMEM((2, 1, rows), jnp.float32),
            pltpu.VMEM((2, rows, LANES), jnp.float32),
            pltpu.VMEM((3, 2, rows, width), jnp.bfloat16),
            pltpu.VMEM((3, 2, 1, rows), jnp.float32),
            dma((4,)),
            dma((3, 2, pieces)),
            dma((3, 2, pieces)),
            dma((3, 2)),
            dma((3, 2)),
            pltpu.SemaphoreType.REGULAR,
        ],
        compiler_params=pltpu.CompilerParams(
            collective_id=0, has_side_effects=True, vmem_limit_bytes=60 * 1024 * 1024
        ),
        cost_estimate=pl.CostEstimate(
            flops=32 * rows * rows * width,
            bytes_accessed=12 * rows * width,
            transcendentals=16 * rows * rows,
        ),
    )(
        logit_scale.reshape(1, 1),
        image_embeds,
        text_embeds,
        image_lse.reshape(1, rows),
        text_lse.reshape(1, rows),
    )
    image_grad = logit_scale * (total[0] - 2.0 * text_embeds.astype(jnp.float32))
    text_grad = logit_scale * (total[1] - 2.0 * image_embeds.astype(jnp.float32))
    return image_grad, text_grad


def solution(mesh):
    return jax.shard_map(
        local,
        mesh=mesh,
        in_specs=(
            P(("outer", "inner"), None),
            P(("outer", "inner"), None),
            P(("outer", "inner")),
            P(("outer", "inner")),
            P(),
        ),
        out_specs=(P(("outer", "inner"), None), P(("outer", "inner"), None)),
        check_vma=False,
    )
```
